1024 devices in a mesh: dp: 16 (over x, y), expert: 64 (over z, core).
Axes of the slice: x: 4, y: 4, z: 32, core: 2. Of those that a mesh axis runs over, the one named last changes fastest.
Arguments:
- tokens: bfloat16 [8192, 6144], P('expert', 'dp'), may hold values from -6 to 6
- cotangent: bfloat16 [8192, 6144], P('expert', 'dp'), may hold values from -6 to 6
- expert_ids: int32 [8192, 8], P('expert'), may hold values from 0 to 127, all different within a row; in each aligned block of 128 rows (0 to 127, 128 to 255, ...) at most 10 rows name the same one
- route_weights: float32 [8192, 8], P('expert'), may hold values from 0.1 to 1
- up_weight: bfloat16 [128, 6144, 1024], P('expert', 'dp'), may hold values from -0.078125 to 0.078125
- down_weight: bfloat16 [128, 1024, 6144], P('expert', None, 'dp'), may hold values from -0.1875 to 0.1875
Outputs:
- critic_out: bfloat16 [8192, 6144], P('expert', 'dp')
- token_grad: bfloat16 [8192, 6144], P('expert', 'dp')
The draws below stay inside these ranges and needn't reach their ends.
Inputs may be any that keep to these rules, and one draw needn't show every extreme that they name: `expert_ids`: each row names 8 different experts. Within every aligned block of 128 rows no expert is named by more than 10 rows, and in some block one expert is named by exactly 10 rows.
All inputs are finite; a program needn't handle non-finite values.
Results may differ from the reference program's by a relative error of at most 0.025.
Values may be sent and summed in bfloat16 or wider, within the bound.
A program may use at most 64 MiB of HBM per device.

```python
import math
import jax
import jax.numpy as jnp
import numpy as np
from jax import lax

D = 6144
FF = 1024
TOP = 8
TOK_DEV = 128
EXPERTS = 128
TOKENS = 8192
CAP = 10
N_DP = 16


def block_scale(own_key, shape, pieces, low, top_value):
    gain = 1.0
    for dim, blocks in pieces:
        draws = jax.random.uniform(jax.random.fold_in(jax.random.fold_in(own_key, 6), dim), (blocks,), jnp.float32, low / len(pieces), top_value / len(pieces))
        gain = gain * jnp.repeat(jnp.exp(draws), shape[dim] // blocks).reshape((-1,) + (1,) * (len(shape) - 1 - dim))
    return gain


def shared_out(own_key, own, number, rows, amount, top, limit, skew):
    sequence = jax.random.permutation(own_key, amount)
    packed, usual = portions_of(amount, rows * top, limit, skew, True), portions_of(amount, rows * top, limit, skew, False)
    places = jnp.arange(amount)

    def named(sizes, turn):
        used = int((sizes > 0).sum())
        fixed = max(1, used // 4)
        shifted = fixed + (places - fixed + turn * (used - fixed)) % max(1, amount - fixed)
        return jnp.zeros((amount,), jnp.int32).at[sequence[jnp.where(places < fixed, places, shifted)]].set(jnp.asarray(sizes, jnp.int32))

    sizes = jnp.where(number % 4 == 0, named(packed, number // 4), named(usual, number - number // 4 - 1))
    mixed = jax.random.permutation(jax.random.fold_in(own, 3), amount)
    donor, receiver = mixed[0:amount // 2 * 2:2], mixed[1:amount // 2 * 2:2]
    slack = jnp.minimum(sizes[donor] - 1, limit - sizes[receiver]) // 2
    slack = jnp.where((donor == sequence[0]) | (receiver == sequence[0]) | (sizes[receiver] == 0), 0, jnp.maximum(slack, 0))
    shifted = jax.random.randint(jax.random.fold_in(own, 4), (amount // 2,), 0, 1 << 20) % (slack + 1)
    sizes = sizes.at[donor].add(-shifted).at[receiver].add(shifted)
    labels = jnp.searchsorted(jnp.cumsum(sizes), jnp.arange(rows * top), side="right").astype(jnp.int32)
    listing = labels.reshape(top, rows).T
    listing = listing[jax.random.permutation(jax.random.fold_in(own, 1), rows)]
    turn = jax.random.randint(jax.random.fold_in(own, 2), (rows, 1), 0, top)
    return jnp.take_along_axis(listing, (jnp.arange(top)[None, :] + turn) % top, axis=1)


def portions_of(count, total, bound, slope, full):
    weights = [(1 << 20) // math.isqrt(rank ** slope) + 1 for rank in range(1, count + 1)]
    largest = bound if full else min(bound, max(-(-total // count), total * weights[0] // sum(weights)))
    least = 1 if total - largest >= count - 1 else 0
    given, surplus = [largest] + [least] * (count - 1), total - largest - least * (count - 1)
    while surplus > 0:
        movable = [i for i in range(1, count) if given[i] < largest] or [i for i in range(1, count) if given[i] < bound]
        mass, remaining = sum([weights[i] for i in movable]), surplus
        for i in movable:
            addition = min(bound - given[i], max(1, remaining * weights[i] // mass), surplus)
            given[i] = given[i] + addition
            surplus = surplus - addition
    return np.array(given)


def bell_draw(rng, shape, spread, limit, cuts=(), kind=jnp.bfloat16):
    values = jax.random.normal(rng, shape, jnp.float32) * spread
    if len(cuts) > 0:
        values = block_scale(rng, shape, cuts, -0.22, 0.18) * values
    return jnp.clip(values, min=-limit, max=limit).astype(kind)


def setup_inputs(seed: int = 0) -> dict:
    key_list = jax.random.split(jax.random.key(seed), 7)
    tokens = bell_draw(key_list[0], (TOKENS, D), 1.0, 6.0, ((0, 64), (1, 16)))
    cotangent = bell_draw(key_list[1], (TOKENS, D), 1.0, 6.0, ((0, 64), (1, 16)))
    expert_ids_keys = jax.random.split(jax.random.fold_in(key_list[2], 1), TOKENS // TOK_DEV)
    expert_ids_turns = jax.random.permutation(jax.random.fold_in(key_list[2], 3), TOKENS // TOK_DEV)
    expert_ids = jax.vmap(lambda own, number: shared_out(jax.random.fold_in(key_list[2], 2), own, number, TOK_DEV, EXPERTS, TOP, CAP, 1))(expert_ids_keys, expert_ids_turns).reshape((TOKENS, TOP))
    route_weights = jnp.clip(0.1 + 0.9 * jax.random.uniform(key_list[3], (TOKENS, TOP), jnp.float32) ** block_scale(key_list[3], (TOKENS, TOP), ((0, 64),), -0.2, 0.2), 0.1, 1.0)
    up_weight = bell_draw(key_list[4], (EXPERTS, D, FF), D ** -0.5, 0.078125, ((0, 64), (1, 16)))
    down_weight = bell_draw(key_list[5], (EXPERTS, FF, D), FF ** -0.5, 0.1875, ((0, 64), (2, 16)))
    return dict(tokens=tokens, cotangent=cotangent, expert_ids=expert_ids, route_weights=route_weights, up_weight=up_weight, down_weight=down_weight)


def silu_slope(pre):
    sigmoid_part = jax.nn.sigmoid(pre)
    return sigmoid_part * (1.0 + pre * (1.0 - sigmoid_part))


def split_product(rows, matrix):
    count = rows.shape[0]
    share = matrix.shape[0] // N_DP
    left = rows.reshape(count, N_DP, share).astype(jnp.float32)
    right = matrix.reshape(N_DP, share, matrix.shape[1]).astype(jnp.float32)
    parts = jnp.einsum("rjd,jdf->rjf", left, right).astype(jnp.bfloat16)
    parts = lax.optimization_barrier(parts)
    return jnp.sum(parts.astype(jnp.float32), axis=1)


def reference(tokens, cotangent, expert_ids, route_weights, up_weight, down_weight):
    blocks = TOKENS // TOK_DEV
    picks = TOK_DEV * TOP
    flat = expert_ids.reshape(blocks, picks)
    onehot = (flat[:, :, None] == jnp.arange(EXPERTS, dtype=jnp.int32)[None, None, :]).astype(jnp.int32)
    earlier = jnp.cumsum(onehot, axis=1) - onehot
    place = jnp.sum(earlier * onehot, axis=2).astype(jnp.int32)
    token_row = (jnp.arange(blocks, dtype=jnp.int32)[:, None] * TOK_DEV
                 + jnp.arange(picks, dtype=jnp.int32)[None, :] // TOP).astype(jnp.int32)
    position = (jnp.arange(blocks, dtype=jnp.int32)[:, None] * CAP + place).astype(jnp.int32)
    table = jnp.zeros((EXPERTS, blocks * CAP), jnp.int32).at[flat, position].set(token_row)
    weight_table = jnp.zeros((EXPERTS, blocks * CAP), jnp.float32).at[flat, position].set(
        route_weights.reshape(blocks, picks).astype(jnp.float32))

    def expert_step(items):
        up, down, rows_idx, slot_weight = items
        x_rows = tokens[rows_idx]
        scaled = (slot_weight[:, None] * cotangent[rows_idx].astype(jnp.float32)).astype(jnp.bfloat16)
        pre = split_product(x_rows, up)
        grad_hidden = split_product(scaled, down.T)
        hidden = jax.nn.silu(pre).astype(jnp.bfloat16)
        grad_pre = (grad_hidden * silu_slope(pre)).astype(jnp.bfloat16)
        out = jnp.dot(hidden, down, preferred_element_type=jnp.float32).astype(jnp.bfloat16)
        back = jnp.dot(grad_pre, up.T, preferred_element_type=jnp.float32).astype(jnp.bfloat16)
        return out, back

    outs, backs = lax.map(expert_step, (up_weight, down_weight, table, weight_table))
    picked_out = outs[flat, position].reshape(TOKENS, TOP, D).astype(jnp.float32)
    picked_back = backs[flat, position].reshape(TOKENS, TOP, D).astype(jnp.float32)
    weights = route_weights[:, :, None].astype(jnp.float32)
    critic_out = jnp.sum(weights * picked_out, axis=1).astype(jnp.bfloat16)
    token_grad = jnp.sum(picked_back, axis=1).astype(jnp.bfloat16)
    return critic_out, token_grad
```

```python
import functools

import jax
import jax.numpy as jnp
from jax import lax
from jax.experimental import pallas as pl
from jax.experimental.pallas import tpu as pltpu
from jax.sharding import PartitionSpec as P

MESH = pl.DeviceIdType.MESH
F32 = jnp.float32
BF16 = jnp.bfloat16
SIDE = 4
CAP = 10


def dot(a, b, ca, cb, precision=None):
    return lax.dot_general(
        a, b, (((ca,), (cb,)), ((), ())), precision=precision, preferred_element_type=F32
    )


def kernel(
    n_chips,
    x_ref, dy_ref, meta_ref, up_hbm, down_hbm, critic_ref, grad_ref,
    up, down, gx, gc, gm, terms, a1, a2, s1, b1, b2, acts, table, slot_w, rx, pc,
    w_sem, ag_send, ag_recv, pair_send, pair_recv, ex_send, ex_recv,
    rs_send, rs_recv, back_send, back_recv,
):
    reach = n_chips // 2
    chunks = reach // 2
    rounds = chunks // 2
    dp, ex = lax.axis_index("dp"), lax.axis_index("expert")
    x, y = lax.div(dp, SIDE), lax.rem(dp, SIDE)
    z, core = lax.div(ex, 2), lax.rem(ex, 2)
    z_up = (dp, lax.rem(z + 1, n_chips) * 2 + core)
    z_down = (dp, lax.rem(z + n_chips - 1, n_chips) * 2 + core)
    partner = (dp, z * 2 + 1 - core)

    def along(axis, step):
        if axis == 0:
            return (lax.rem(x + step, SIDE) * SIDE + y, ex)
        return (x * SIDE + lax.rem(y + step, SIDE), ex)

    weights_in = (
        pltpu.make_async_copy(up_hbm, up, w_sem.at[0]),
        pltpu.make_async_copy(down_hbm, down, w_sem.at[1]),
    )
    for copy in weights_in:
        copy.start()

    barrier = pltpu.get_barrier_semaphore()
    others = (z_up, z_down, partner, along(0, 1), along(0, 3), along(1, 1), along(1, 3))
    for device in others:
        pl.semaphore_signal(barrier, inc=1, device_id=device, device_id_type=MESH)
    pl.semaphore_wait(barrier, len(others))

    def remote(src, dst, send, recv, device):
        return pltpu.make_async_remote_copy(
            src_ref=src, dst_ref=dst, send_sem=send, recv_sem=recv,
            device_id=device, device_id_type=MESH,
        )

    def pair_no(distance, way):
        return (distance - 1) * 2 + way

    gathered = (gx, gc, gm)
    own = pair_no(reach, 1)

    def to_chip(stream, src, dst, device):
        g = gathered[stream]
        return remote(
            g.at[2 * src], g.at[2 * dst], ag_send.at[stream, dst], ag_recv.at[stream, dst], device
        )

    def to_partner(stream, no):
        g = gathered[stream]
        return remote(
            g.at[2 * no], g.at[2 * no + 1], pair_send.at[stream, no], pair_recv.at[stream, no],
            partner,
        )

    gx[2 * own] = x_ref[...]
    gc[2 * own] = dy_ref[...]
    gm[2 * own] = meta_ref[...]
    for stream in range(3):
        to_chip(stream, own, pair_no(1, 0), z_up).start()
        to_chip(stream, own, pair_no(1, 1), z_down).start()
    for stream in range(3):
        to_partner(stream, own).start()

    def gather_tick(distance):
        for stream in range(3):
            for way, device in ((0, z_up), (1, z_down)):
                no = pair_no(distance, way)

                def arrive():
                    to_chip(stream, no, no, device).wait_recv()

                    @pl.when(distance < reach - way)
                    def _():
                        to_chip(stream, no, no + 2, device).start()

                    to_partner(stream, no).start()

                if way == 0:
                    arrive()
                else:
                    pl.when(distance < reach)(arrive)

    def chunk_terms(k):
        i, half = lax.div(k, 2), lax.rem(k, 2)
        for stream in range(3):
            for no in range(4):
                to_partner(stream, 4 * k + no).wait_recv()
        meta = gm[pl.ds(8 * k, 8)]
        ids, route = meta[:, :8, :], meta[:, 8:, :]
        rows = 8 * CAP
        before = (
            lax.broadcasted_iota(jnp.int32, (128, 128), 0)
            < lax.broadcasted_iota(jnp.int32, (128, 128), 1)
        ).astype(F32).astype(BF16)
        row = lax.broadcasted_iota(jnp.int32, (rows, 128), 0)
        block_of = lax.shift_right_logical(row * 205, 11)
        place = (row - block_of * CAP).astype(F32)
        row8 = lax.broadcasted_iota(jnp.int32, (rows, 8), 0)
        spread = (
            lax.shift_right_logical(row8 * 205, 11)
            == lax.broadcasted_iota(jnp.int32, (rows, 8), 1)
        ).astype(F32)
        tables, weights = [], []
        for e in range(2):
            hit = ids == (2 * ex + e).astype(F32)
            sel = jnp.sum(jnp.where(hit, 1.0, 0.0), axis=1)
            weight = jnp.sum(jnp.where(hit, route, 0.0), axis=1)
            rank = dot(sel.astype(BF16), before, 1, 0)
            sel_rows = dot(spread.astype(BF16), sel.astype(BF16), 1, 0)
            rank_rows = dot(spread.astype(BF16), rank.astype(BF16), 1, 0)
            weight_rows = dot(spread, weight, 1, 0, lax.Precision.HIGHEST)
            taken = jnp.where((sel_rows > 0.5) & (rank_rows == place), 1.0, 0.0)
            weights.append(jnp.sum(taken * weight_rows, axis=1, keepdims=True))
            tables.append(
                jnp.concatenate(
                    [jnp.where(block_of == b, taken, 0.0) for b in range(8)], axis=1
                ).astype(BF16)
            )
        whole = jnp.concatenate(tables, axis=0)
        slot_weight = jnp.concatenate(weights, axis=0)
        table[k] = whole
        slot_w[k] = jnp.broadcast_to(slot_weight, (2 * rows, 128))
        picked_x = dot(whole, gx[pl.ds(8 * k, 8)].reshape(1024, -1), 1, 0).astype(BF16)
        picked_dy = (
            dot(whole, gc[pl.ds(8 * k, 8)].reshape(1024, -1), 1, 0) * slot_weight
        ).astype(BF16)
        for e in range(2):
            span = slice(rows * e, rows * (e + 1))
            pre = dot(picked_x[span], up[e], 1, 0).astype(BF16)
            slope = dot(picked_dy[span], down[e], 1, 1).astype(BF16)
            for q in range(4):
                for c in range(2):
                    lanes = slice(256 * q + 128 * c, 256 * q + 128 * (c + 1))
                    terms[i, e, q, 2 * half + c, 0] = pre[:, lanes]
                    terms[i, e, q, 2 * half + c, 1] = slope[:, lanes]

    def places(e):
        first, second = (x, y) if e == 0 else (y, x)

        def near(p):
            return lax.rem(p + 1, SIDE), lax.rem(p + 2, SIDE), lax.rem(p + 3, SIDE)

        return first, near(first), second, near(second)

    def hop(i, e, step, way, src, dst):
        axis = e if step in (0, 1, 6, 7) else 1 - e
        return remote(
            src, dst, ex_send.at[i, e, step, way], ex_recv.at[i, e, step, way],
            along(axis, 1 if way == 0 else 3),
        )

    def plus(a, b):
        return (a.astype(F32) + b.astype(F32)).astype(BF16)

    def exchange(step, i):
        for e in range(2):
            p1, (r1, o1, l1), p2, (r2, o2, l2) = places(e)
            t, s, h = terms.at[i, e], s1.at[i, e], acts.at[i, e]
            if step == 0:
                hop(i, e, 0, 0, t.at[o1, pl.ds(0, 2)], a1.at[i, e, 0]).start()
                hop(i, e, 0, 1, t.at[o1, pl.ds(2, 2)], a1.at[i, e, 1]).start()
            elif step == 1:
                for way, p in ((0, r1), (1, l1)):
                    hop(i, e, 0, way, a1.at[i, e, way], a1.at[i, e, way]).wait_recv()
                    for n in range(2):
                        m = 2 * way + n
                        terms[i, e, p, m] = plus(terms[i, e, p, m], a1[i, e, way, n])
                    hop(i, e, 1, way, t.at[p], a2.at[i, e, way]).start()
            elif step == 2:
                for way in range(2):
                    hop(i, e, 1, way, a2.at[i, e, way], a2.at[i, e, way]).wait_recv()
                for n in range(4):
                    s1[i, e, n] = (
                        terms[i, e, p1, n].astype(F32)
                        + a2[i, e, 0, n].astype(F32)
                        + a2[i, e, 1, n].astype(F32)
                    ).astype(BF16)
                for way in range(2):
                    hop(i, e, 2, way, s.at[o2, way], b1.at[i, e, way]).start()
            elif step == 3:
                for way, p in ((0, r2), (1, l2)):
                    hop(i, e, 2, way, b1.at[i, e, way], b1.at[i, e, way]).wait_recv()
                    s1[i, e, p, way] = plus(s1[i, e, p, way], b1[i, e, way])
                    hop(i, e, 3, way, s.at[p], b2.at[i, e, way]).start()
            elif step == 4:
                for way in range(2):
                    hop(i, e, 3, way, b2.at[i, e, way], b2.at[i, e, way]).wait_recv()
                total = (
                    s1[i, e, p2].astype(F32)
                    + b2[i, e, 0].astype(F32)
                    + b2[i, e, 1].astype(F32)
                )
                pre, grad_hidden = total[0], total[1]
                gate = 1.0 / (1.0 + jnp.exp(-pre))
                acts[i, e, p1, p2, 0] = (pre * gate).astype(BF16)
                acts[i, e, p1, p2, 1] = (
                    grad_hidden * (gate * (1.0 + pre * (1.0 - gate)))
                ).astype(BF16)
                for way in range(2):
                    hop(i, e, 4, way, h.at[p1, p2], h.at[p1, p2]).start()
            elif step == 5:
                for way, p in ((0, l2), (1, r2)):
                    hop(i, e, 4, way, h.at[p1, p], h.at[p1, p]).wait_recv()
                    hop(i, e, 5, way, h.at[p1, p, way], h.at[p1, p, way]).start()
            elif step == 6:
                for way in range(2):
                    hop(i, e, 5, way, h.at[p1, o2, way], h.at[p1, o2, way]).wait_recv()
                for way in range(2):
                    hop(i, e, 6, way, h.at[p1], h.at[p1]).start()
            elif step == 7:
                for way, p in ((0, l1), (1, r1)):
                    hop(i, e, 6, way, h.at[p], h.at[p]).wait_recv()
                    part = h.at[p, pl.ds(2 * way, 2)]
                    hop(i, e, 7, way, part, part).start()
            else:
                for way in range(2):
                    part = h.at[o1, pl.ds(2 * way, 2)]
                    hop(i, e, 7, way, part, part).wait_recv()

    for copy in weights_in:
        copy.wait()

    def tick(t, carry):
        pl.when(t <= reach)(lambda: gather_tick(t))

        def at(step):
            after = t - 5 - step

            @pl.when((after >= 0) & (lax.rem(after, 4) == 0) & (after < 4 * rounds))
            def _():
                exchange(step, lax.div(after, 4))

        for step in range(8, 0, -1):
            at(step)

        @pl.when((t >= 3) & (lax.rem(t, 2) == 1) & (t <= 2 * chunks + 1))
        def _():
            chunk_terms(lax.div(t - 3, 2))

        at(0)
        return carry

    lax.fori_loop(1, 4 * rounds + 10, tick, 0)

    def sent_all(no, carry):
        for stream in range(3):
            pl.when(no != own)(lambda: to_chip(stream, no, no, z_up).wait_send())
            to_partner(stream, no).wait_send()
        return carry

    lax.fori_loop(0, 2 * reach, sent_all, 0)

    def partner_share(stream, no):
        return remote(
            gathered[stream].at[2 * no + 1], pc.at[stream, no],
            back_send.at[stream, no], back_recv.at[stream, no], partner,
        )

    def running_sum(stream, no, to, device):
        return remote(
            gathered[stream].at[2 * no], rx.at[stream, to],
            rs_send.at[stream, to], rs_recv.at[stream, to], device,
        )

    def project(k):
        i, half = lax.div(k, 2), lax.rem(k, 2)
        rows = 8 * CAP
        outs, backs = [], []
        for e in range(2):
            hidden, grad_pre = (
                jnp.concatenate(
                    [acts[i, e, q, 2 * half + c, n] for q in range(4) for c in range(2)], axis=1
                )
                for n in range(2)
            )
            weight = slot_w[k, pl.ds(rows * e, rows)]
            weight = jnp.concatenate([weight] * (down.shape[2] // 128), axis=1)
            outs.append((dot(hidden, down[e], 1, 0) * weight).astype(BF16))
            backs.append(dot(grad_pre, up[e], 1, 1).astype(BF16))
        out = jnp.concatenate(outs, axis=0)
        back = jnp.concatenate(backs, axis=0)
        for b in range(8):
            chosen = table[k, :, pl.ds(128 * b, 128)]
            gx[8 * k + b] = dot(chosen, out, 0, 0).astype(BF16)
            gc[8 * k + b] = dot(chosen, back, 0, 0).astype(BF16)

    def reduce_tick(distance):
        for stream in range(2):
            g = gathered[stream]
            for way, device in ((0, z_down), (1, z_up)):
                no = pair_no(distance, way)

                def add():
                    partner_share(stream, no).wait_recv()
                    mine = g[2 * no].astype(F32) + pc[stream, no].astype(F32)
                    first = distance == reach - way

                    @pl.when(first)
                    def _():
                        g[2 * no] = mine.astype(BF16)

                    @pl.when(jnp.logical_not(first))
                    def _():
                        at = 2 * distance + way
                        running_sum(stream, no, at, device).wait_recv()
                        total = g[2 * no].astype(F32) + pc[stream, no].astype(F32)
                        g[2 * no] = (total + rx[stream, at].astype(F32)).astype(BF16)

                    running_sum(stream, no, 2 * distance - 2 + way, device).start()

                if way == 0:
                    add()
                else:
                    pl.when(distance < reach)(add)

    def back_step(n, carry):
        k = chunks - 1 - n
        project(k)
        for no in range(4):
            for stream in range(2):
                partner_share(stream, 4 * k + no).start()
        reduce_tick(2 * k + 2)
        reduce_tick(2 * k + 1)
        return carry

    lax.fori_loop(0, chunks, back_step, 0)

    for stream, out_ref in ((0, critic_ref), (1, grad_ref)):
        partner_share(stream, own).wait_recv()
        total = gathered[stream][2 * own].astype(F32) + pc[stream, own].astype(F32)
        for way, device in ((0, z_down), (1, z_up)):
            running_sum(stream, own, way, device).wait_recv()
            total = total + rx[stream, way].astype(F32)
        out_ref[...] = total.astype(BF16)

    def drain_back(no, carry):
        for stream in range(2):
            partner_share(stream, no).wait_send()
            pl.when(no < 2 * reach - 1)(
                lambda: running_sum(stream, no, no, z_up).wait_send()
            )
        return carry

    lax.fori_loop(0, 2 * reach, drain_back, 0)

    for i in range(rounds):
        for e in range(2):
            t, s, h = terms.at[i, e], s1.at[i, e], acts.at[i, e]
            sizes = (
                t.at[0, pl.ds(0, 2)], t.at[0], s.at[0, 0], s.at[0],
                h.at[0, 0], h.at[0, 0, 0], h.at[0], h.at[0, pl.ds(0, 2)],
            )
            for step in range(8):
                for way in range(2):
                    hop(i, e, step, way, sizes[step], sizes[step]).wait_send()


def solution(mesh):
    n_chips = mesh.shape["expert"] // 2
    reach = n_chips // 2
    chunks = reach // 2
    rounds = chunks // 2

    def local(tokens, cotangent, expert_ids, route_weights, up_weight, down_weight):
        count, width = tokens.shape
        units = up_weight.shape[2]
        meta = jnp.concatenate([expert_ids.T.astype(F32), route_weights.T], axis=0)
        rows = 8 * CAP
        vmem = pltpu.VMEM
        dma = pltpu.SemaphoreType.DMA
        pairs = 2 * reach
        shape = jax.ShapeDtypeStruct((count, width), BF16)
        critic_out, token_grad = pl.pallas_call(
            functools.partial(kernel, n_chips),
            out_shape=(shape, shape),
            in_specs=[pl.BlockSpec(memory_space=pltpu.VMEM)] * 3
            + [pl.BlockSpec(memory_space=pl.ANY)] * 2,
            out_specs=(pl.BlockSpec(memory_space=pltpu.VMEM),) * 2,
            scratch_shapes=[
                vmem((2, width, units), BF16),
                vmem((2, units, width), BF16),
                vmem((2 * pairs, count, width), BF16),
                vmem((2 * pairs, count, width), BF16),
                vmem((2 * pairs, 16, count), F32),
                vmem((rounds, 2, 4, 4, 2, rows, 128), BF16),
                vmem((rounds, 2, 2, 2, 2, rows, 128), BF16),
                vmem((rounds, 2, 2, 4, 2, rows, 128), BF16),
                vmem((rounds, 2, 4, 2, rows, 128), BF16),
                vmem((rounds, 2, 2, rows, 128), BF16),
                vmem((rounds, 2, 2, 2, rows, 128), BF16),
                vmem((rounds, 2, 4, 4, 2, rows, 128), BF16),
                vmem((chunks, 2 * rows, 8 * count), BF16),
                vmem((chunks, 2 * rows, 128), F32),
                vmem((2, pairs, count, width), BF16),
                vmem((2, pairs, count, width), BF16),
                dma((2,)),
                dma((3, pairs)), dma((3, pairs)), dma((3, pairs)), dma((3, pairs)),
                dma((rounds, 2, 8, 2)), dma((rounds, 2, 8, 2)),
                dma((2, pairs)), dma((2, pairs)), dma((2, pairs)), dma((2, pairs)),
            ],
            compiler_params=pltpu.CompilerParams(
                collective_id=0, has_side_effects=True, vmem_limit_bytes=62 * 1024 * 1024
            ),
        )(tokens, cotangent, meta, up_weight, down_weight)
        return critic_out, token_grad

    in_specs = (
        P("expert", "dp"),
        P("expert", "dp"),
        P("expert", None),
        P("expert", None),
        P("expert", "dp", None),
        P("expert", None, "dp"),
    )
    out_specs = (P("expert", "dp"), P("expert", "dp"))
    return jax.shard_map(local, mesh=mesh, in_specs=in_specs, out_specs=out_specs, check_vma=False)
```

```python
import functools

import jax
import jax.numpy as jnp
from jax import lax
from jax.experimental import pallas as pl
from jax.experimental.pallas import tpu as pltpu
from jax.sharding import PartitionSpec as P

MESH = pl.DeviceIdType.MESH
F32 = jnp.float32
BF16 = jnp.bfloat16
SIDE = 4
CAP = 10


def dot(a, b, ca, cb, precision=None):
    return lax.dot_general(
        a, b, (((ca,), (cb,)), ((), ())), precision=precision, preferred_element_type=F32
    )


def kernel(
    n_chips,
    x_ref, dy_ref, ids_ref, route_ref, up_hbm, down_hbm, critic_ref, grad_ref,
    up, down, gx, gc, gm, terms, a1, a2, s1, b1, b2, acts, table, slot_w, picked, rx, pc,
    w_sem, ag_send, ag_recv, pair_send, pair_recv, ex_send, ex_recv,
    rs_send, rs_recv, back_send, back_recv,
):
    reach = n_chips // 2
    chunks = reach // 2
    rounds = chunks // 2
    dp, ex = lax.axis_index("dp"), lax.axis_index("expert")
    x, y = lax.div(dp, SIDE), lax.rem(dp, SIDE)
    z, core = lax.div(ex, 2), lax.rem(ex, 2)
    z_up = (dp, lax.rem(z + 1, n_chips) * 2 + core)
    z_down = (dp, lax.rem(z + n_chips - 1, n_chips) * 2 + core)
    partner = (dp, z * 2 + 1 - core)

    def along(axis, step):
        if axis == 0:
            return (lax.rem(x + step, SIDE) * SIDE + y, ex)
        return (x * SIDE + lax.rem(y + step, SIDE), ex)

    weights_in = (
        pltpu.make_async_copy(up_hbm, up, w_sem.at[0]),
        pltpu.make_async_copy(down_hbm, down, w_sem.at[1]),
    )
    for copy in weights_in:
        copy.start()

    barrier = pltpu.get_barrier_semaphore()
    others = (z_up, z_down, partner, along(0, 1), along(0, 3), along(1, 1), along(1, 3))
    for device in others:
        pl.semaphore_signal(barrier, inc=1, device_id=device, device_id_type=MESH)
    pl.semaphore_wait(barrier, len(others))

    def remote(src, dst, send, recv, device):
        return pltpu.make_async_remote_copy(
            src_ref=src, dst_ref=dst, send_sem=send, recv_sem=recv,
            device_id=device, device_id_type=MESH,
        )

    def pair_no(distance, way):
        return (distance - 1) * 2 + way

    gathered = (gx, gc, gm)
    own = pair_no(reach, 1)
    part_rows = x_ref.shape[0] // 2

    def piece(number, slot):
        if number == 4:
            return gm.at[slot]
        return gathered[number // 2].at[slot, pl.ds(number % 2 * part_rows, part_rows)]

    def to_chip(number, src, dst, device):
        return remote(
            piece(number, 2 * src), piece(number, 2 * dst),
            ag_send.at[number, dst], ag_recv.at[number, dst], device,
        )

    def to_partner(stream, no):
        g = gathered[stream]
        return remote(
            g.at[2 * no], g.at[2 * no + 1], pair_send.at[stream, no], pair_recv.at[stream, no],
            partner,
        )

    gx[2 * own] = x_ref[...]
    gc[2 * own] = dy_ref[...]
    gm[2 * own] = jnp.concatenate([ids_ref[...].astype(F32), route_ref[...]], axis=0)
    for number in range(5):
        to_chip(number, own, pair_no(1, 0), z_up).start()
        to_chip(number, own, pair_no(1, 1), z_down).start()
    for stream in range(3):
        to_partner(stream, own).start()

    def far_way(stream):
        return 1 if stream == 1 else 0

    def gather_piece(number, distance):
        for way, device in ((0, z_up), (1, z_down)):
            no = pair_no(distance, way)

            def arrive():
                to_chip(number, no, no, device).wait_recv()

                if way == far_way(number // 2):

                    @pl.when(distance < reach)
                    def _():
                        step = 2 if way == 0 else jnp.where(distance == reach - 1, 1, 2)
                        to_chip(number, no, no + step, device).start()

                else:

                    @pl.when(distance < reach - 1)
                    def _():
                        to_chip(number, no, no + 2, device).start()

                if number in (1, 3, 4):
                    to_partner(number // 2, no).start()

            pl.when(distance <= reach - way)(arrive)

    def chunk_part(part, k):
        i, half = lax.div(k, 2), lax.rem(k, 2)
        rows = 8 * CAP
        if part in (0, 2, 3):
            stream = (2, None, 0, 1)[part]
            for no in range(4):
                to_partner(stream, 4 * k + no).wait_recv()
        if part < 2:
            e = part
            meta = gm[pl.ds(8 * k, 8)]
            ids, route = meta[:, :8, :], meta[:, 8:, :]
            before = (
                lax.broadcasted_iota(jnp.int32, (128, 128), 0)
                < lax.broadcasted_iota(jnp.int32, (128, 128), 1)
            ).astype(F32).astype(BF16)
            row = lax.broadcasted_iota(jnp.int32, (rows, 128), 0)
            block_of = lax.shift_right_logical(row * 205, 11)
            place = (row - block_of * CAP).astype(F32)
            row8 = lax.broadcasted_iota(jnp.int32, (rows, 8), 0)
            spread = (
                lax.shift_right_logical(row8 * 205, 11)
                == lax.broadcasted_iota(jnp.int32, (rows, 8), 1)
            ).astype(F32)
            hit = ids == (2 * ex + e).astype(F32)
            sel = jnp.sum(jnp.where(hit, 1.0, 0.0), axis=1)
            weight = jnp.sum(jnp.where(hit, route, 0.0), axis=1)
            rank = dot(sel.astype(BF16), before, 1, 0)
            sel_rows = dot(spread.astype(BF16), sel.astype(BF16), 1, 0)
            rank_rows = dot(spread.astype(BF16), rank.astype(BF16), 1, 0)
            weight_rows = dot(spread, weight, 1, 0, lax.Precision.HIGHEST)
            taken = jnp.where((sel_rows > 0.5) & (rank_rows == place), 1.0, 0.0)
            slot_weight = jnp.sum(taken * weight_rows, axis=1, keepdims=True)
            table[k, rows * e : rows * (e + 1)] = jnp.concatenate(
                [jnp.where(block_of == b, taken, 0.0) for b in range(8)], axis=1
            ).astype(BF16)
            slot_w[k, rows * e : rows * (e + 1)] = jnp.broadcast_to(slot_weight, (rows, 128))
        elif part == 2:
            picked[0] = dot(table[k], gx[pl.ds(8 * k, 8)].reshape(1024, -1), 1, 0).astype(BF16)
        elif part == 3:
            rows_dy = dot(table[k], gc[pl.ds(8 * k, 8)].reshape(1024, -1), 1, 0)
            weight = jnp.concatenate([slot_w[k]] * (rows_dy.shape[1] // 128), axis=1)
            picked[1] = (rows_dy * weight).astype(BF16)
        else:
            e, kind = (part - 4) // 2, part % 2
            lhs = picked[kind, rows * e : rows * (e + 1)]
            product = (dot(lhs, down[e], 1, 1) if kind else dot(lhs, up[e], 1, 0)).astype(BF16)
            for q in range(4):
                for c in range(2):
                    lanes = slice(256 * q + 128 * c, 256 * q + 128 * (c + 1))
                    terms[i, e, q, 2 * half + c, kind] = product[:, lanes]

    def places(e):
        first, second = (x, y) if e == 0 else (y, x)

        def near(p):
            return lax.rem(p + 1, SIDE), lax.rem(p + 2, SIDE), lax.rem(p + 3, SIDE)

        return first, near(first), second, near(second)

    def hop(i, e, step, way, src, dst):
        axis = e if step in (0, 1, 6, 7) else 1 - e
        return remote(
            src, dst, ex_send.at[i, e, step, way], ex_recv.at[i, e, step, way],
            along(axis, 1 if way == 0 else 3),
        )

    def plus(a, b):
        return (a.astype(F32) + b.astype(F32)).astype(BF16)

    def exchange(step, i):
        for e in range(2):
            p1, (r1, o1, l1), p2, (r2, o2, l2) = places(e)
            t, s, h = terms.at[i, e], s1.at[i, e], acts.at[i, e]
            if step == 0:
                hop(i, e, 0, 0, t.at[o1, pl.ds(0, 2)], a1.at[i, e, 0]).start()
                hop(i, e, 0, 1, t.at[o1, pl.ds(2, 2)], a1.at[i, e, 1]).start()
            elif step == 1:
                for way, p in ((0, r1), (1, l1)):
                    hop(i, e, 0, way, a1.at[i, e, way], a1.at[i, e, way]).wait_recv()
                    for n in range(2):
                        m = 2 * way + n
                        terms[i, e, p, m] = plus(terms[i, e, p, m], a1[i, e, way, n])
                    hop(i, e, 1, way, t.at[p], a2.at[i, e, way]).start()
            elif step == 2:
                for way in range(2):
                    hop(i, e, 1, way, a2.at[i, e, way], a2.at[i, e, way]).wait_recv()
                for n in range(4):
                    s1[i, e, n] = (
                        terms[i, e, p1, n].astype(F32)
                        + a2[i, e, 0, n].astype(F32)
                        + a2[i, e, 1, n].astype(F32)
                    ).astype(BF16)
                for way in range(2):
                    hop(i, e, 2, way, s.at[o2, way], b1.at[i, e, way]).start()
            elif step == 3:
                for way, p in ((0, r2), (1, l2)):
                    hop(i, e, 2, way, b1.at[i, e, way], b1.at[i, e, way]).wait_recv()
                    s1[i, e, p, way] = plus(s1[i, e, p, way], b1[i, e, way])
                    hop(i, e, 3, way, s.at[p], b2.at[i, e, way]).start()
            elif step == 4:
                for way in range(2):
                    hop(i, e, 3, way, b2.at[i, e, way], b2.at[i, e, way]).wait_recv()
                total = (
                    s1[i, e, p2].astype(F32)
                    + b2[i, e, 0].astype(F32)
                    + b2[i, e, 1].astype(F32)
                )
                pre, grad_hidden = total[0], total[1]
                gate = 1.0 / (1.0 + jnp.exp(-pre))
                acts[i, e, p1, p2, 0] = (pre * gate).astype(BF16)
                acts[i, e, p1, p2, 1] = (
                    grad_hidden * (gate * (1.0 + pre * (1.0 - gate)))
                ).astype(BF16)
                for way in range(2):
                    hop(i, e, 4, way, h.at[p1, p2], h.at[p1, p2]).start()
            elif step == 5:
                for way, p in ((0, l2), (1, r2)):
                    hop(i, e, 4, way, h.at[p1, p], h.at[p1, p]).wait_recv()
                    hop(i, e, 5, way, h.at[p1, p, way], h.at[p1, p, way]).start()
            elif step == 6:
                for way in range(2):
                    hop(i, e, 5, way, h.at[p1, o2, way], h.at[p1, o2, way]).wait_recv()
                for way in range(2):
                    hop(i, e, 6, way, h.at[p1], h.at[p1]).start()
            elif step == 7:
                for way, p in ((0, l1), (1, r1)):
                    hop(i, e, 6, way, h.at[p], h.at[p]).wait_recv()
                    part = h.at[p, pl.ds(2 * way, 2)]
                    hop(i, e, 7, way, part, part).start()
            else:
                for way in range(2):
                    part = h.at[o1, pl.ds(2 * way, 2)]
                    hop(i, e, 7, way, part, part).wait_recv()

    for copy in weights_in:
        copy.wait()

    def tick(t, carry):
        def at(step):
            after = t - 6 - (0, 1, 3, 4, 5, 6, 7, 9, 10)[step]

            @pl.when((after >= 0) & (lax.rem(after, 4) == 0) & (after < 4 * rounds))
            def _():
                exchange(step, lax.div(after, 4))

        odd = lax.rem(t, 2) == 1
        for number in range(5):
            pl.when(t <= reach)(lambda: gather_piece(number, t))
            for step in ((8, 7), (6, 5), (4, 3), (2, 1), ())[number]:
                at(step)
            if number < 4:

                @pl.when((t >= 3) & odd & (t <= 2 * chunks + 1))
                def _():
                    chunk_part(number, lax.div(t - 3, 2))

                @pl.when((t >= 4) & jnp.logical_not(odd) & (t <= 2 * chunks + 2))
                def _():
                    chunk_part(4 + number, lax.div(t - 4, 2))

        at(0)

        @pl.when(t == reach + 1)
        def _():
            lax.fori_loop(0, 2 * reach, sent_all, 0)

        @pl.when((t >= reach + 4) & (t <= reach + chunks + 1))
        def _():
            project(t - reach - 4)

        return carry

    def sent_all(no, carry):
        for number in range(5):
            pl.when(no != own)(lambda: to_chip(number, no, no, z_up).wait_send())
        for stream in range(3):
            to_partner(stream, no).wait_send()
        return carry

    def partner_share(stream, no):
        return remote(
            gathered[stream].at[2 * no + 1], pc.at[stream, no],
            back_send.at[stream, no], back_recv.at[stream, no], partner,
        )

    def running_sum(number, no, to, device):
        rows = pl.ds(number % 2 * part_rows, part_rows)
        return remote(
            gathered[number // 2].at[2 * no, rows], rx.at[number // 2, to, rows],
            rs_send.at[number, to], rs_recv.at[number, to], device,
        )

    def project(k):
        i, half = lax.div(k, 2), lax.rem(k, 2)
        rows = 8 * CAP
        outs, backs = [], []
        for e in range(2):
            hidden, grad_pre = (
                jnp.concatenate(
                    [acts[i, e, q, 2 * half + c, n] for q in range(4) for c in range(2)], axis=1
                )
                for n in range(2)
            )
            weight = slot_w[k, pl.ds(rows * e, rows)]
            weight = jnp.concatenate([weight] * (down.shape[2] // 128), axis=1)
            outs.append((dot(hidden, down[e], 1, 0) * weight).astype(BF16))
            backs.append(dot(grad_pre, up[e], 1, 1).astype(BF16))
        out = jnp.concatenate(outs, axis=0)
        back = jnp.concatenate(backs, axis=0)
        for b in range(8):
            chosen = table[k, :, pl.ds(128 * b, 128)]
            gx[8 * k + b] = dot(chosen, out, 0, 0).astype(BF16)
            gc[8 * k + b] = dot(chosen, back, 0, 0).astype(BF16)
        for no in range(4):
            for stream in range(2):
                partner_share(stream, 4 * k + no).start()

    lax.fori_loop(1, 4 * rounds + 13, tick, 0)

    def reduce_tick(distance):
        for number in range(4):
            stream = number // 2
            g = gathered[stream]
            rows = pl.ds(number % 2 * part_rows, part_rows)
            for way, device in ((0, z_down), (1, z_up)):
                far = way == far_way(stream)
                no = pair_no(distance, way)
                if far and way == 1:
                    no = jnp.where(distance == reach, no - 1, no)

                def add():
                    if number % 2 == 0:
                        partner_share(stream, no).wait_recv()
                    first = distance == (reach if far else reach - 1)

                    @pl.when(first)
                    def _():
                        mine = g[2 * no, rows].astype(F32) + pc[stream, no, rows].astype(F32)
                        g[2 * no, rows] = mine.astype(BF16)

                    @pl.when(jnp.logical_not(first))
                    def _():
                        at = 2 * distance + way
                        running_sum(number, no, at, device).wait_recv()
                        total = g[2 * no, rows].astype(F32) + pc[stream, no, rows].astype(F32)
                        g[2 * no, rows] = (total + rx[stream, at, rows].astype(F32)).astype(BF16)

                    running_sum(number, no, 2 * distance - 2 + way, device).start()

                if far:
                    add()
                else:
                    pl.when(distance < reach)(add)

    def back_step(n, carry):
        k = chunks - 1 - n
        pl.when(n < 2)(lambda: project(k))
        reduce_tick(2 * k + 2)
        reduce_tick(2 * k + 1)
        return carry

    lax.fori_loop(0, chunks, back_step, 0)

    for stream, out_ref in ((0, critic_ref), (1, grad_ref)):
        partner_share(stream, own).wait_recv()
        total = gathered[stream][2 * own].astype(F32) + pc[stream, own].astype(F32)
        for way, device in ((0, z_down), (1, z_up)):
            for half in range(2):
                running_sum(2 * stream + half, own, way, device).wait_recv()
            total = total + rx[stream, way].astype(F32)
        out_ref[...] = total.astype(BF16)

    def drain_back(no, carry):
        for stream in range(2):
            partner_share(stream, no).wait_send()
        for number in range(4):
            unused = 2 * reach - 1 - far_way(number // 2)
            pl.when(no != unused)(lambda: running_sum(number, no, no, z_up).wait_send())
        return carry

    lax.fori_loop(0, 2 * reach, drain_back, 0)

    for i in range(rounds):
        for e in range(2):
            t, s, h = terms.at[i, e], s1.at[i, e], acts.at[i, e]
            sizes = (
                t.at[0, pl.ds(0, 2)], t.at[0], s.at[0, 0], s.at[0],
                h.at[0, 0], h.at[0, 0, 0], h.at[0], h.at[0, pl.ds(0, 2)],
            )
            for step in range(8):
                for way in range(2):
                    hop(i, e, step, way, sizes[step], sizes[step]).wait_send()


def solution(mesh):
    n_chips = mesh.shape["expert"] // 2
    reach = n_chips // 2
    chunks = reach // 2
    rounds = chunks // 2

    def local(tokens, cotangent, expert_ids, route_weights, up_weight, down_weight):
        count, width = tokens.shape
        units = up_weight.shape[2]
        rows = 8 * CAP
        vmem = pltpu.VMEM
        dma = pltpu.SemaphoreType.DMA
        pairs = 2 * reach
        shape = jax.ShapeDtypeStruct((count, width), BF16)
        critic_out, token_grad = pl.pallas_call(
            functools.partial(kernel, n_chips),
            out_shape=(shape, shape),
            in_specs=[pl.BlockSpec(memory_space=pltpu.VMEM)] * 4
            + [pl.BlockSpec(memory_space=pl.ANY)] * 2,
            out_specs=(pl.BlockSpec(memory_space=pltpu.VMEM),) * 2,
            scratch_shapes=[
                vmem((2, width, units), BF16),
                vmem((2, units, width), BF16),
                vmem((2 * pairs, count, width), BF16),
                vmem((2 * pairs, count, width), BF16),
                vmem((2 * pairs, 16, count), F32),
                vmem((rounds, 2, 4, 4, 2, rows, 128), BF16),
                vmem((rounds, 2, 2, 2, 2, rows, 128), BF16),
                vmem((rounds, 2, 2, 4, 2, rows, 128), BF16),
                vmem((rounds, 2, 4, 2, rows, 128), BF16),
                vmem((rounds, 2, 2, rows, 128), BF16),
                vmem((rounds, 2, 2, 2, rows, 128), BF16),
                vmem((rounds, 2, 4, 4, 2, rows, 128), BF16),
                vmem((chunks, 2 * rows, 8 * count), BF16),
                vmem((chunks, 2 * rows, 128), F32),
                vmem((2, 2 * rows, width), BF16),
                vmem((2, pairs, count, width), BF16),
                vmem((2, pairs, count, width), BF16),
                dma((2,)),
                dma((5, pairs)), dma((5, pairs)), dma((3, pairs)), dma((3, pairs)),
                dma((rounds, 2, 8, 2)), dma((rounds, 2, 8, 2)),
                dma((4, pairs)), dma((4, pairs)), dma((2, pairs)), dma((2, pairs)),
            ],
            compiler_params=pltpu.CompilerParams(
                collective_id=0, has_side_effects=True, vmem_limit_bytes=62 * 1024 * 1024
            ),
        )(tokens, cotangent, expert_ids.T, route_weights.T, up_weight, down_weight)
        return critic_out, token_grad

    in_specs = (
        P("expert", "dp"),
        P("expert", "dp"),
        P("expert", None),
        P("expert", None),
        P("expert", "dp", None),
        P("expert", None, "dp"),
    )
    out_specs = (P("expert", "dp"), P("expert", "dp"))
    return jax.shard_map(local, mesh=mesh, in_specs=in_specs, out_specs=out_specs, check_vma=False)
```
